128 devices in a mesh: user: 16 (over y_lo, z, core), item: 8 (over y_hi, x).
Axes of the slice: x: 4, y: 4 (y_hi: 2, y_lo: 2; y = y_hi * 2 + y_lo), z: 4, core: 2. Of those that a mesh axis runs over, the one named last changes fastest.
Arguments:
- confidence: bfloat16 [16384, 65536], P('user', 'item'), may hold values from 0 to 20, as said below
- item_factors: bfloat16 [65536, 128], P(('item', 'user')), may hold values from -6 to 6
- user_factors: float32 [16384, 128], P(('user', 'item')), may hold values from -0.5 to 0.5
- precond: float32 [128, 128], replicated, may hold values from -0.00390625 to 0.5, as said below
Outputs:
- updated_users: float32 [16384, 128], P(('user', 'item'))
The draws below stay inside these ranges and needn't reach their ends.
Inputs may be any that keep to these rules, and one draw needn't show every extreme that they name: `confidence`: zero or between 1 and 20. `precond`: diagonally dominant with a positive diagonal.
All inputs are finite; a program needn't handle non-finite values.
Results may differ from the reference program's by a relative error of at most 0.0025.
Values may be sent and summed in bfloat16 or wider, within the bound.
A program may use at most 64 MiB of HBM per device.

```python
import math
import jax
import jax.numpy as jnp
from jax import lax

K = 128
U_DEV = 1024
TURNS = 2
USERS = 16384
ITEMS = 65536


def draw_confidence(key, part):
    key = jax.random.fold_in(key, 1)
    key_density, key_pick, key_value = jax.random.split(key, 3)
    density = jnp.exp(jax.random.uniform(key_density, (USERS, 1), jnp.float32, math.log(0.03), math.log(0.3)))
    ramp = 0.5 + jnp.arange(ITEMS, dtype=jnp.float32) / ITEMS
    observed = jax.random.uniform(key_pick, (USERS, ITEMS), jnp.float32) < density * ramp[None, :]
    value = jnp.exp(jax.random.uniform(key_value, (USERS, ITEMS), jnp.float32, 0.0, math.log(20.0)))
    return jnp.where(observed, value, 0.0).astype(jnp.bfloat16)


def draw_precond(key, part):
    key = jax.random.fold_in(key, 2)
    key_diag, key_off = jax.random.split(key)
    diagonal = jax.random.uniform(key_diag, (K,), jnp.float32, 0.6, 1.0)
    spread = jax.random.uniform(key_off, (K, K), jnp.float32, -1.0, 1.0) / K
    index_row = jnp.arange(K)[:, None]
    index_col = jnp.arange(K)[None, :]
    matrix = jnp.where(index_row == index_col, diagonal[:, None] * jnp.ones((K, K), jnp.float32), spread)
    return (0.4375 * matrix).astype(jnp.float32)


def shard_levels(rng, dims, shards, smallest, high):
    loudness = 1.0
    for position, shards_of in shards:
        draws = jax.random.uniform(jax.random.fold_in(jax.random.fold_in(rng, 6), position), (shards_of,), jnp.float32, smallest / len(shards), high / len(shards))
        loudness = loudness * jnp.repeat(jnp.exp(draws), dims[position] // shards_of).reshape((-1,) + (1,) * (len(dims) - 1 - position))
    return loudness


def gaussian(stream_key, shape, width, reach, pieces=(), held_as=jnp.bfloat16):
    drawn = width * jax.random.normal(stream_key, shape, jnp.float32)
    if pieces:
        drawn = drawn * shard_levels(stream_key, shape, pieces, -0.22, 0.18)
    return jnp.clip(drawn, -reach, reach).astype(held_as)


def setup_inputs(seed: int = 0) -> dict:
    keys = jax.random.split(jax.random.key(seed), 5)
    return {
        "confidence": draw_confidence(jax.random.fold_in(keys[4], 71), 0),
        "item_factors": gaussian(keys[1], (ITEMS, K), 1.0, 6.0, ((0, 128),)),
        "user_factors": gaussian(keys[2], (USERS, K), K ** -0.5, 0.5, ((0, 128),), jnp.float32),
        "precond": draw_precond(jax.random.fold_in(keys[4], 71), 0),
    }


prior_weight = 64.0
gram_coef = 0.5
ridge_coef = 0.1


def reference(confidence, item_factors, user_factors, precond):
    gram_matrix = jnp.dot(item_factors.T, item_factors, preferred_element_type=jnp.float32)
    row_weight = jnp.sum(confidence.astype(jnp.float32), axis=1) + prior_weight
    factors = user_factors
    groups = USERS // U_DEV
    blocked = confidence.reshape(groups, U_DEV, ITEMS)
    for sweep in range(TURNS):
        factors_bf = factors.astype(jnp.bfloat16).reshape(groups, U_DEV, K)

        def per_block(pair):
            conf_block, rows_bf = pair
            scores = jnp.dot(rows_bf, item_factors.T, preferred_element_type=jnp.float32)
            residual = (conf_block.astype(jnp.float32) * (scores - 1.0)).astype(jnp.bfloat16)
            return jnp.dot(residual, item_factors, preferred_element_type=jnp.float32)

        products = lax.map(per_block, (blocked, factors_bf)).reshape(USERS, K)
        gradient = products / row_weight[:, None]
        gradient = gradient + (gram_coef / ITEMS) * jnp.dot(factors, gram_matrix, precision=lax.Precision.HIGHEST)
        gradient = gradient + ridge_coef * factors
        factors = factors - jnp.dot(gradient, precond, precision=lax.Precision.HIGHEST)
    return factors
```

```python
import jax
import jax.numpy as jnp
from jax import lax
from jax.experimental import pallas as pl
from jax.experimental.pallas import tpu as pltpu
from jax.sharding import PartitionSpec as P

K = 128
ITEMS = 65536
prior_weight = 64.0
gram_coef = 0.5
ridge_coef = 0.1

BF = jnp.bfloat16
F32 = jnp.float32
HIGHEST = lax.Precision.HIGHEST
MESH = pl.DeviceIdType.MESH

OWNERS = ((0, 0), (0, 1), (0, 3), (1, 0), (0, 2), (1, 1), (1, 3), (1, 2))
CHIPS = ((0, 0), (1, 0), (0, 1), (0, 3), (0, 2), (1, 1), (1, 3), (1, 2))


def mirrored(table):
    return tuple(table.index((a, (4 - b) % 4)) for a, b in table)


OWNER_BACK = mirrored(OWNERS)
CHIP_BACK = mirrored(CHIPS)

FIRST_ORDER = (7, 5, 6, 3, 4, 1, 2, 0)
SECOND_ORDER = (0, 1, 7, 5, 6, 3, 4, 2)
LATE_CHIP = 4


def kernel(
    conf_hbm, items, users, precond, out,
    conf, table, rows, total, sums, gram, parts, shares, weight_out, weight_in,
    conf_sem, item_send, item_recv, pair_send, pair_recv,
    row_send, row_recv, part_send, part_recv, weight_send, weight_recv,
):
    user = lax.axis_index("user")
    item = lax.axis_index("item")
    core, z, y = user % 2, (user // 2) % 4, user // 8
    x, half = item % 4, item // 4
    pair = (user + 1 - 2 * core, item)

    def owner(k):
        dh, dx = OWNERS[k]
        return (half + dh) % 2 * 4 + (x + dx) % 4

    def chip(j):
        dy, dz = CHIPS[j]
        return (y + dy) % 2 * 4 + (z + dz) % 4

    peers = [(user, owner(k)) for k in range(8)]
    mates = [(chip(j) * 2 + core, item) for j in range(8)]

    barrier = pltpu.get_barrier_semaphore()
    for device in [pair] + peers[1:] + mates[1:]:
        pl.semaphore_signal(barrier, inc=1, device_id=device, device_id_type=MESH)

    def conf_copy(j, k):
        source = conf_hbm.at[
            pl.ds(pl.multiple_of(owner(k) * 128, 128), 128),
            pl.ds(pl.multiple_of(chip(j) * 1024, 1024), 1024),
        ]
        return pltpu.make_async_copy(
            source, conf.at[k, :, pl.ds(j * 1024, 1024)], conf_sem.at[j, k]
        )

    for j in range(8):
        for k in range(8):
            conf_copy(j, k).start()

    mine = pl.ds(pl.multiple_of(core * 512, 512), 512)
    table[0, mine, :] = items[...]
    rows[0, 0] = users[...].astype(BF)
    sums[...] = jnp.zeros_like(sums)

    def row_copy(turn, k):
        back = OWNER_BACK[k]
        return pltpu.make_async_remote_copy(
            src_ref=rows.at[turn, 0], dst_ref=rows.at[turn, back],
            send_sem=row_send.at[turn, k], recv_sem=row_recv.at[turn, back],
            device_id=peers[k], device_id_type=MESH,
        )

    def item_copy(j):
        back = CHIP_BACK[j]
        return pltpu.make_async_remote_copy(
            src_ref=items, dst_ref=table.at[back, mine],
            send_sem=item_send.at[j], recv_sem=item_recv.at[back],
            device_id=mates[j], device_id_type=MESH,
        )

    def pair_copy(j):
        return pltpu.make_async_remote_copy(
            src_ref=items if j == 0 else table.at[j, mine], dst_ref=table.at[j, mine],
            send_sem=pair_send.at[j], recv_sem=pair_recv.at[j],
            device_id=pair, device_id_type=MESH,
        )

    def part_copy(turn, k):
        back = OWNER_BACK[k]
        return pltpu.make_async_remote_copy(
            src_ref=parts.at[turn, k], dst_ref=shares.at[turn, back],
            send_sem=part_send.at[turn, k], recv_sem=part_recv.at[turn, back],
            device_id=peers[k], device_id_type=MESH,
        )

    def weight_copy(k):
        back = OWNER_BACK[k]
        return pltpu.make_async_remote_copy(
            src_ref=weight_out.at[k], dst_ref=weight_in.at[back],
            send_sem=weight_send.at[k], recv_sem=weight_recv.at[back],
            device_id=peers[k], device_id_type=MESH,
        )

    pl.semaphore_wait(barrier, 15)
    pair_copy(0).start()
    for k in range(1, 8):
        row_copy(0, k).start()
    for j in range(1, 8):
        item_copy(j).start()

    def items_of(first, last):
        return table[first:last].reshape((last - first) * 1024, K)

    def products(turn, k0, k1, first, last, weigh):
        users_here = rows[turn, k0:k1].reshape((k1 - k0) * 128, K)
        block = items_of(first, last)
        tile = conf[k0:k1, :, first * 1024:last * 1024].reshape(
            (k1 - k0) * 128, (last - first) * 1024
        ).astype(F32)
        scores = lax.dot_general(
            users_here, block, (((1,), (1,)), ((), ())), preferred_element_type=F32
        )
        residual = (tile * (scores - 1.0)).astype(BF)
        if weigh:
            folded = tile[:, :K]
            for n in range(1, (last - first) * 8):
                folded = folded + tile[:, n * K:(n + 1) * K]
            sums[k0:k1] = sums[k0:k1] + folded.reshape(k1 - k0, 128, K)
        return jnp.dot(residual, block, preferred_element_type=F32)

    def gram_of(first, last):
        block = items_of(first, last)
        return lax.dot_general(
            block, block, (((0,), (0,)), ((), ())), preferred_element_type=F32
        )

    def forward(first, last):
        for j in range(first, last):
            item_copy(CHIP_BACK[j]).wait_recv()
            pair_copy(j).start()

    for k in range(1, 8):
        row_copy(0, OWNER_BACK[k]).wait_recv()
    pair_copy(0).wait_recv()
    for k in range(8):
        conf_copy(0, k).wait()
    total[...] = products(0, 0, 8, 0, 1, True).reshape(8, 128, K)
    gram[...] = gram_of(0, 1)
    forward(1, LATE_CHIP)
    for j in range(1, LATE_CHIP):
        pair_copy(j).wait_recv()
        for k in range(8):
            conf_copy(j, k).wait()
        total[...] = total[...] + products(0, 0, 8, j, j + 1, True).reshape(8, 128, K)
        gram[...] = gram[...] + gram_of(j, j + 1)
    forward(LATE_CHIP, 8)
    for j in range(LATE_CHIP, 8):
        pair_copy(j).wait_recv()
        for k in range(8):
            conf_copy(j, k).wait()
    scaled = (gram[...] + gram_of(LATE_CHIP, 8)) * (gram_coef / ITEMS)
    high = scaled.astype(BF)
    low = (scaled - high.astype(F32)).astype(BF)
    both = jnp.concatenate([high, low], axis=1)

    def gram_rows(turn, k):
        wide = jnp.dot(rows[turn, k], both, preferred_element_type=F32)
        return wide[:, :K] + wide[:, K:]

    def weight_of(k):
        return lax.dot_general(
            jnp.ones((8, K), F32), sums[k], (((1,), (1,)), ((), ())),
            precision=HIGHEST, preferred_element_type=F32,
        )

    own_part = own_gram = own_weight = None
    for k in FIRST_ORDER:
        part = total[k] + products(0, k, k + 1, LATE_CHIP, 8, True)
        if k == 0:
            own_part, own_gram, own_weight = part, gram_rows(0, k), weight_of(k)
        else:
            weight_out[k] = weight_of(k)
            weight_copy(k).start()
            parts[0, k, 0] = part.astype(BF)
            parts[0, k, 1] = gram_rows(0, k).astype(BF)
            part_copy(0, k).start()

    for k in range(1, 8):
        weight_copy(OWNER_BACK[k]).wait_recv()
        own_weight = own_weight + weight_in[k]
    weight = jnp.transpose(jnp.broadcast_to(own_weight[0:1] + prior_weight, (128, K)))

    def step(turn, factors, part, gram_part):
        for k in range(1, 8):
            part_copy(turn, OWNER_BACK[k]).wait_recv()
            part = part + shares[turn, k, 0].astype(F32)
            gram_part = gram_part + shares[turn, k, 1].astype(F32)
        gradient = part / weight + gram_part + ridge_coef * factors
        return factors - jnp.dot(
            gradient, precond[...], precision=HIGHEST, preferred_element_type=F32
        )

    factors = step(0, users[...], own_part, own_gram)
    rows[1, 0] = factors.astype(BF)
    for k in range(1, 8):
        row_copy(1, k).start()

    for k in SECOND_ORDER:
        if k:
            row_copy(1, OWNER_BACK[k]).wait_recv()
        part = products(1, k, k + 1, 0, 8, False)
        if k == 0:
            own_part, own_gram = part, gram_rows(1, k)
        else:
            parts[1, k, 0] = part.astype(BF)
            parts[1, k, 1] = gram_rows(1, k).astype(BF)
            part_copy(1, k).start()
    out[...] = step(1, factors, own_part, own_gram)

    pair_copy(0).wait_send()
    for k in range(1, 8):
        item_copy(k).wait_send()
        pair_copy(k).wait_send()
        weight_copy(k).wait_send()
        for turn in range(2):
            row_copy(turn, k).wait_send()
            part_copy(turn, k).wait_send()


def shards(confidence, item_factors, user_factors, precond):
    vmem = pl.BlockSpec(memory_space=pltpu.VMEM)
    dma = pltpu.SemaphoreType.DMA
    return pl.pallas_call(
        kernel,
        name="user_half_step",
        out_shape=jax.ShapeDtypeStruct(user_factors.shape, F32),
        in_specs=[pl.BlockSpec(memory_space=pl.ANY), vmem, vmem, vmem],
        out_specs=vmem,
        scratch_shapes=[
            pltpu.VMEM((8, 128, 8192), BF),
            pltpu.VMEM((8, 1024, K), BF),
            pltpu.VMEM((2, 8, 128, K), BF),
            pltpu.VMEM((8, 128, K), F32),
            pltpu.VMEM((8, 128, K), F32),
            pltpu.VMEM((K, K), F32),
            pltpu.VMEM((2, 8, 2, 128, K), BF),
            pltpu.VMEM((2, 8, 2, 128, K), BF),
            pltpu.VMEM((8, 8, K), F32),
            pltpu.VMEM((8, 8, K), F32),
            dma((8, 8)), dma((8,)), dma((8,)), dma((8,)), dma((8,)),
            dma((2, 8)), dma((2, 8)), dma((2, 8)), dma((2, 8)), dma((8,)), dma((8,)),
        ],
        compiler_params=pltpu.CompilerParams(
            collective_id=0, has_side_effects=True, vmem_limit_bytes=56 * 2**20
        ),
        cost_estimate=pl.CostEstimate(
            flops=4 * 2 * 1024 * 8192 * 128, bytes_accessed=17 * 2**20, transcendentals=0
        ),
    )(confidence, item_factors, user_factors, precond)


def solution(mesh):
    return jax.shard_map(
        shards,
        mesh=mesh,
        in_specs=(P("user", "item"), P(("item", "user"), None), P(("user", "item"), None), P()),
        out_specs=P(("user", "item"), None),
        check_vma=False,
    )
```

```python
import jax
import jax.numpy as jnp
from jax import lax
from jax.experimental import pallas as pl
from jax.experimental.pallas import tpu as pltpu
from jax.sharding import PartitionSpec as P

K = 128
ITEMS = 65536
prior_weight = 64.0
gram_coef = 0.5
ridge_coef = 0.1

BF = jnp.bfloat16
F32 = jnp.float32
HIGHEST = lax.Precision.HIGHEST
MESH = pl.DeviceIdType.MESH

OWNERS = ((0, 0), (0, 1), (0, 3), (1, 0), (0, 2), (1, 1), (1, 3), (1, 2))
CHIPS = ((0, 0), (1, 0), (0, 1), (0, 3), (0, 2), (1, 1), (1, 3), (1, 2))


def mirrored(table):
    return tuple(table.index((a, (4 - b) % 4)) for a, b in table)


OWNER_BACK = mirrored(OWNERS)
NEAR = (1, 2, 3, 4)
FAR = (5, 6, 7)
VIA = 3
PASS_ON = {1: 6, 2: 5, 4: 7}
PASSED_BY = {6: 1, 5: 2, 7: 4}
CHIP_BACK = mirrored(CHIPS)

FIRST_ORDER = (7, 5, 6, 3, 4, 1, 2, 0)
SECOND_ORDER = (0, 1, 3, 5, 7, 6, 4, 2)
DIRECT = (1, 2, 3)
FORWARD = (
    (2, 256, 512, 4, 0, 3),
    (3, 0, 256, 4, 4, 2),
    (1, 0, 512, 6, 6, 2),
    (1, 0, 512, 5, 5, 3),
    (4, 0, 512, 7, 7, 1),
)
LATE = 5
GROUPS = ((0, 1), (1, 4), (4, 5), (5, 8))
SOON = 3
SHIFT = 0.1875


def kernel(
    conf_hbm, items_hbm, users_hbm, precond_hbm, out,
    conf, table, users, precond, rows, total, sums, inverse, parts, shares,
    weight_out, weight_in, conf_sem, local_sem, item_send, item_recv, on_send, pair_send,
    pair_recv, row_send, row_recv, part_send, part_recv, weight_send, weight_recv,
    pass_send,
):
    user = lax.axis_index("user")
    item = lax.axis_index("item")
    core, z, y = user % 2, (user // 2) % 4, user // 8
    x, half = item % 4, item // 4
    pair = (user + 1 - 2 * core, item)

    def owner(k):
        dh, dx = OWNERS[k]
        return (half + dh) % 2 * 4 + (x + dx) % 4

    def chip(j):
        dy, dz = CHIPS[j]
        return (y + dy) % 2 * 4 + (z + dz) % 4

    peers = [(user, owner(k)) for k in range(8)]
    mates = [(chip(j) * 2 + core, item) for j in range(8)]

    barrier = pltpu.get_barrier_semaphore()
    greeted = [pair] + [peers[k] for k in NEAR] + [mates[j] for j in DIRECT]
    for device in greeted:
        pl.semaphore_signal(barrier, inc=1, device_id=device, device_id_type=MESH)

    mine = pl.ds(pl.multiple_of(core * 512, 512), 512)
    own_items = pltpu.make_async_copy(items_hbm, table.at[0, mine], local_sem.at[0])
    own_users = pltpu.make_async_copy(users_hbm, users, local_sem.at[1])
    own_precond = pltpu.make_async_copy(precond_hbm, precond, local_sem.at[2])
    own_users.start()
    own_items.start()
    own_precond.start()

    def conf_copy(j, k):
        source = conf_hbm.at[
            pl.ds(pl.multiple_of(owner(k) * 128, 128), 128),
            pl.ds(pl.multiple_of(chip(j) * 1024, 1024), 1024),
        ]
        return pltpu.make_async_copy(
            source, conf.at[k, :, pl.ds(j * 1024, 1024)], conf_sem.at[j, k]
        )

    def load_conf(first, last):
        for j in range(first, last):
            for k in range(8):
                conf_copy(j, k).start()

    load_conf(0, SOON)

    def remote(source, target, send_sem, recv_sem, device):
        return pltpu.make_async_remote_copy(
            src_ref=source, dst_ref=target, send_sem=send_sem, recv_sem=recv_sem,
            device_id=device, device_id_type=MESH,
        )

    def row_copy(turn, k):
        back = OWNER_BACK[k]
        return remote(
            rows.at[turn, 0], rows.at[turn, back],
            row_send.at[turn, k], row_recv.at[turn, back], peers[k],
        )

    def row_pass(k):
        to = PASS_ON[k]
        return remote(
            rows.at[0, VIA], rows.at[0, to], pass_send.at[0, k], row_recv.at[0, to], peers[k]
        )

    def item_copy(j):
        back = CHIP_BACK[j]
        return remote(
            table.at[0, mine], table.at[back, mine], item_send.at[j], item_recv.at[back], mates[j]
        )

    def on_copy(n):
        source, first, last, to, sem, mate = FORWARD[n]
        part = pl.ds(pl.multiple_of(core * 512 + first, 256), last - first)
        return remote(
            table.at[source, part], table.at[to, part],
            on_send.at[n], item_recv.at[sem], mates[mate],
        )

    def pair_copy(g):
        first, last = GROUPS[g]
        return remote(
            table.at[first:last, mine], table.at[first:last, mine],
            pair_send.at[g], pair_recv.at[g], pair,
        )

    def part_copy(turn, k):
        back = OWNER_BACK[k]
        return remote(
            parts.at[turn, k], shares.at[turn, back],
            part_send.at[turn, k], part_recv.at[turn, back], peers[k],
        )

    def weight_copy(k):
        back = OWNER_BACK[k]
        return remote(
            weight_out, weight_in.at[back], weight_send.at[k], weight_recv.at[back], peers[k]
        )

    def weight_pass(k):
        to = PASS_ON[k]
        return remote(
            weight_in.at[VIA], weight_in.at[to], pass_send.at[1, k], weight_recv.at[to], peers[k]
        )

    def add_weights(first, last):
        for j in range(first, last):
            for k in range(8):
                conf_copy(j, k).wait()

            def one(k, carry):
                folded = sums[k]
                for n in range(j * 8, j * 8 + 8):
                    folded = folded + conf[k, :, n * K:(n + 1) * K].astype(F32)
                sums[k] = folded
                return carry

            lax.fori_loop(0, 8, one, 0)

    own_users.wait()
    rows[0, 0] = users[...].astype(BF)
    own_items.wait()
    own_precond.wait()

    pl.semaphore_wait(barrier, len(greeted))
    for k in NEAR:
        row_copy(0, k).start()
    pair_copy(0).start()
    for j in DIRECT[:3]:
        item_copy(j).start()
    load_conf(SOON, 8)
    sums[...] = jnp.zeros_like(sums)
    add_weights(0, SOON)

    def items_of(first, last):
        return table[first:last].reshape((last - first) * 1024, K)

    def products(turn, k0, k1, first, last):
        users_here = rows[turn, k0:k1].reshape((k1 - k0) * 128, K)
        block = items_of(first, last)
        tile = conf[k0:k1, :, first * 1024:last * 1024].reshape(
            (k1 - k0) * 128, (last - first) * 1024
        ).astype(F32)
        scores = lax.dot_general(
            users_here, block, (((1,), (1,)), ((), ())), preferred_element_type=F32
        )
        residual = (tile * (scores - 1.0)).astype(BF)
        done = jnp.dot(residual, block, preferred_element_type=F32)
        return done.reshape(k1 - k0, 128, K)

    def gram_of(first, last):
        block = items_of(first, last)
        return lax.dot_general(
            block, block, (((0,), (0,)), ((), ())), preferred_element_type=F32
        )

    def rows_arrive(turn, *ks):
        for k in ks:
            if turn == 0 and k in FAR:
                row_pass(PASSED_BY[k]).wait_recv()
            else:
                row_copy(turn, OWNER_BACK[k]).wait_recv()

    rows_arrive(0, 1, 2)
    pair_copy(0).wait_recv()
    total[0:3] = products(0, 0, 3, 0, 1)
    rows_arrive(0, VIA)
    for k in PASS_ON:
        row_pass(k).start()
    for j in (2, 3, 1):
        item_copy(CHIP_BACK[j]).wait_recv()
        for n in range(4):
            if FORWARD[n][0] == j:
                on_copy(n).start()
    pair_copy(1).start()

    add_weights(SOON, 8)
    line = lax.broadcasted_iota(jnp.int32, (8, K), 0)
    own_weight = jnp.zeros((8, K), F32)
    for k in range(8):
        summed = lax.dot_general(
            jnp.ones((8, K), F32), sums[k], (((1,), (1,)), ((), ())),
            precision=HIGHEST, preferred_element_type=F32,
        )
        own_weight = jnp.where(line == owner(k), summed, own_weight)
    weight_out[...] = own_weight
    for k in NEAR:
        weight_copy(k).start()

    gram = gram_of(0, 1)
    for n in (0, 1):
        on_copy(n).wait_recv()
    on_copy(4).start()
    pair_copy(2).start()
    pair_copy(1).wait_recv()
    total[0:3] = total[0:3] + products(0, 0, 3, 1, 4)
    rows_arrive(0, *FAR)
    rows_arrive(0, 4)
    weight_copy(OWNER_BACK[VIA]).wait_recv()
    for k in PASS_ON:
        weight_pass(k).start()
    total[3:5] = products(0, 3, 5, 0, 4)
    total[5:8] = products(0, 5, 8, 0, 4)
    for n in (2, 3, 4):
        on_copy(n).wait_recv()
    pair_copy(3).start()
    pair_copy(2).wait_recv()
    total[...] = total[...] + products(0, 0, 8, 4, 5)
    gram = gram + gram_of(1, 5)

    for k in range(1, 8):
        if k in FAR:
            weight_pass(PASSED_BY[k]).wait_recv()
        elif k != VIA:
            weight_copy(OWNER_BACK[k]).wait_recv()
        own_weight = own_weight + weight_in[k]
    reciprocal = 1.0 / (own_weight + prior_weight)
    for k in range(8):
        picked = jnp.sum(jnp.where(line == owner(k), reciprocal, 0.0), axis=0, keepdims=True)
        inverse[k] = jnp.transpose(jnp.broadcast_to(picked, (128, K)))

    pair_copy(3).wait_recv()
    gram = (gram + gram_of(LATE, 8)) * (gram_coef / ITEMS)
    high = gram.astype(BF)
    low = (gram - high.astype(F32)).astype(BF)
    both = jnp.concatenate([high, low], axis=1)

    def part_of(turn, k, product):
        wide = jnp.dot(rows[turn, k], both, preferred_element_type=F32)
        return product * inverse[k] + (wide[:, :K] + wide[:, K:])

    def hand_out(turn, k, product):
        part = part_of(turn, k, product)
        parts[turn, k] = (part - SHIFT * rows[turn, k].astype(F32)).astype(BF)
        part_copy(turn, k).start()

    def step(turn, factors, gradient):
        gradient = gradient + ridge_coef * factors
        gradient = gradient + (7 * SHIFT) * rows[turn, 0].astype(F32)
        for k in FIRST_ORDER[:7]:
            part_copy(turn, OWNER_BACK[k]).wait_recv()
            gradient = gradient + shares[turn, k].astype(F32)
        return factors - jnp.dot(
            gradient, precond[...], precision=HIGHEST, preferred_element_type=F32
        )

    for k in FIRST_ORDER:
        product = total[k] + products(0, k, k + 1, LATE, 8)[0]
        if k:
            hand_out(0, k, product)
        else:
            own = part_of(0, 0, product)
    factors = step(0, users[...], own)
    rows[1, 0] = factors.astype(BF)
    for k in range(1, 8):
        row_copy(1, k).start()

    for k in SECOND_ORDER:
        if k:
            rows_arrive(1, k)
        product = products(1, k, k + 1, 0, 8)[0]
        if k:
            hand_out(1, k, product)
        else:
            own = part_of(1, 0, product)
    out[...] = step(1, factors, own)

    for g in range(len(GROUPS)):
        pair_copy(g).wait_send()
    for j in DIRECT:
        item_copy(j).wait_send()
    for n in range(len(FORWARD)):
        on_copy(n).wait_send()
    for k in PASS_ON:
        row_pass(k).wait_send()
        weight_pass(k).wait_send()
    for k in NEAR:
        weight_copy(k).wait_send()
        row_copy(0, k).wait_send()
    for k in range(1, 8):
        row_copy(1, k).wait_send()
        for turn in range(2):
            part_copy(turn, k).wait_send()


def shards(confidence, item_factors, user_factors, precond):
    dma = pltpu.SemaphoreType.DMA
    return pl.pallas_call(
        kernel,
        name="user_half_step",
        out_shape=jax.ShapeDtypeStruct(user_factors.shape, F32),
        in_specs=[pl.BlockSpec(memory_space=pl.ANY)] * 4,
        out_specs=pl.BlockSpec(memory_space=pltpu.VMEM),
        scratch_shapes=[
            pltpu.VMEM((8, 128, 8192), BF),
            pltpu.VMEM((8, 1024, K), BF),
            pltpu.VMEM((128, K), F32),
            pltpu.VMEM((K, K), F32),
            pltpu.VMEM((2, 8, 128, K), BF),
            pltpu.VMEM((8, 128, K), F32),
            pltpu.VMEM((8, 128, K), F32),
            pltpu.VMEM((8, 128, K), F32),
            pltpu.VMEM((2, 8, 128, K), BF),
            pltpu.VMEM((2, 8, 128, K), BF),
            pltpu.VMEM((8, K), F32),
            pltpu.VMEM((8, 8, K), F32),
            dma((8, 8)), dma((3,)), dma((8,)), dma((8,)), dma((8,)), dma((8,)),
            dma((8,)), dma((2, 8)), dma((2, 8)), dma((2, 8)), dma((2, 8)), dma((8,)), dma((8,)),
            dma((2, 8)),
        ],
        compiler_params=pltpu.CompilerParams(
            collective_id=0, has_side_effects=True, vmem_limit_bytes=56 * 2**20
        ),
        cost_estimate=pl.CostEstimate(
            flops=4 * 2 * 1024 * 8192 * 128, bytes_accessed=17 * 2**20, transcendentals=0
        ),
    )(confidence, item_factors, user_factors, precond)


def solution(mesh):
    return jax.shard_map(
        shards,
        mesh=mesh,
        in_specs=(P("user", "item"), P(("item", "user"), None), P(("user", "item"), None), P()),
        out_specs=P(("user", "item"), None),
        check_vma=False,
    )
```

```python
import jax
import jax.numpy as jnp
from jax import lax
from jax.experimental import pallas as pl
from jax.experimental.pallas import tpu as pltpu
from jax.sharding import PartitionSpec as P

K = 128
ITEMS = 65536
prior_weight = 64.0
gram_coef = 0.5
ridge_coef = 0.1

BF = jnp.bfloat16
F32 = jnp.float32
HIGHEST = lax.Precision.HIGHEST
MESH = pl.DeviceIdType.MESH

OWNERS = ((0, 0), (0, 1), (0, 3), (1, 0), (0, 2), (1, 1), (1, 3), (1, 2))
CHIPS = ((0, 0), (1, 0), (0, 1), (0, 3), (0, 2), (1, 1), (1, 3), (1, 2))


def mirrored(table):
    return tuple(table.index((a, (4 - b) % 4)) for a, b in table)


OWNER_BACK = mirrored(OWNERS)
NEAR = (1, 2, 3, 4)
FAR = (5, 6, 7)
VIA = 3
PASS_ON = {1: 6, 2: 5, 4: 7}
PASSED_BY = {6: 1, 5: 2, 7: 4}
CHIP_BACK = mirrored(CHIPS)

FIRST_ORDER = (7, 5, 6, 3, 4, 1, 2, 0)
SECOND_ORDER = (0, 1, 3, 5, 7, 6, 4, 2)
DIRECT = (1, 2, 3)
FORWARD = (
    (2, 256, 512, 4, 0, 3),
    (3, 0, 256, 4, 4, 2),
    (1, 0, 512, 6, 6, 2),
    (1, 0, 512, 5, 5, 3),
    (4, 0, 512, 7, 7, 1),
)
LATE = 5
GROUPS = ((0, 1), (1, 4), (4, 5), (5, 8))
SOON = 3
SHIFT = 0.1875


def kernel(
    conf_hbm, items_hbm, users_hbm, precond_hbm, out,
    conf, table, users, precond, rows, total, sums, inverse, parts, shares,
    weight_out, weight_in, conf_sem, local_sem, item_send, item_recv, on_send, pair_send,
    pair_recv, row_send, row_recv, part_send, part_recv, weight_send, weight_recv,
    pass_send,
):
    user = lax.axis_index("user")
    item = lax.axis_index("item")
    core, z, y = user % 2, (user // 2) % 4, user // 8
    x, half = item % 4, item // 4
    pair = (user + 1 - 2 * core, item)

    def owner(k):
        dh, dx = OWNERS[k]
        return (half + dh) % 2 * 4 + (x + dx) % 4

    def chip(j):
        dy, dz = CHIPS[j]
        return (y + dy) % 2 * 4 + (z + dz) % 4

    peers = [(user, owner(k)) for k in range(8)]
    mates = [(chip(j) * 2 + core, item) for j in range(8)]

    barrier = pltpu.get_barrier_semaphore()
    greeted = [pair] + [peers[k] for k in NEAR] + [mates[j] for j in DIRECT]
    for device in greeted:
        pl.semaphore_signal(barrier, inc=1, device_id=device, device_id_type=MESH)

    mine = pl.ds(pl.multiple_of(core * 512, 512), 512)
    own_items = pltpu.make_async_copy(items_hbm, table.at[0, mine], local_sem.at[0])
    own_users = pltpu.make_async_copy(users_hbm, users, local_sem.at[1])
    own_precond = pltpu.make_async_copy(precond_hbm, precond, local_sem.at[2])
    own_users.start()
    own_items.start()
    own_precond.start()

    def conf_copy(j, k):
        source = conf_hbm.at[
            pl.ds(pl.multiple_of(owner(k) * 128, 128), 128),
            pl.ds(pl.multiple_of(chip(j) * 1024, 1024), 1024),
        ]
        return pltpu.make_async_copy(
            source, conf.at[k, :, pl.ds(j * 1024, 1024)], conf_sem.at[j, k]
        )

    def load_conf(first, last):
        for j in range(first, last):
            for k in range(8):
                conf_copy(j, k).start()

    load_conf(0, SOON)

    def remote(source, target, send_sem, recv_sem, device):
        return pltpu.make_async_remote_copy(
            src_ref=source, dst_ref=target, send_sem=send_sem, recv_sem=recv_sem,
            device_id=device, device_id_type=MESH,
        )

    def row_copy(turn, k):
        back = OWNER_BACK[k]
        return remote(
            rows.at[turn, 0], rows.at[turn, back],
            row_send.at[turn, k], row_recv.at[turn, back], peers[k],
        )

    def row_pass(k):
        to = PASS_ON[k]
        return remote(
            rows.at[0, VIA], rows.at[0, to], pass_send.at[0, k], row_recv.at[0, to], peers[k]
        )

    def item_copy(j):
        back = CHIP_BACK[j]
        return remote(
            table.at[0, mine], table.at[back, mine], item_send.at[j], item_recv.at[back], mates[j]
        )

    def on_copy(n):
        source, first, last, to, sem, mate = FORWARD[n]
        part = pl.ds(pl.multiple_of(core * 512 + first, 256), last - first)
        return remote(
            table.at[source, part], table.at[to, part],
            on_send.at[n], item_recv.at[sem], mates[mate],
        )

    def pair_copy(g):
        first, last = GROUPS[g]
        return remote(
            table.at[first:last, mine], table.at[first:last, mine],
            pair_send.at[g], pair_recv.at[g], pair,
        )

    def part_copy(turn, k):
        back = OWNER_BACK[k]
        return remote(
            parts.at[turn, k], shares.at[turn, back],
            part_send.at[turn, k], part_recv.at[turn, back], peers[k],
        )

    def weight_copy(k):
        back = OWNER_BACK[k]
        return remote(
            weight_out, weight_in.at[back], weight_send.at[k], weight_recv.at[back], peers[k]
        )

    def weight_pass(k):
        to = PASS_ON[k]
        return remote(
            weight_in.at[VIA], weight_in.at[to], pass_send.at[1, k], weight_recv.at[to], peers[k]
        )

    def add_weights(first, last):
        for j in range(first, last):
            for k in range(8):
                conf_copy(j, k).wait()

            def one(k, carry):
                folded = sums[k]
                for n in range(j * 8, j * 8 + 8):
                    folded = folded + conf[k, :, n * K:(n + 1) * K].astype(F32)
                sums[k] = folded
                return carry

            lax.fori_loop(0, 8, one, 0)

    own_users.wait()
    rows[0, 0] = users[...].astype(BF)
    own_items.wait()
    own_precond.wait()

    pl.semaphore_wait(barrier, len(greeted))
    for k in NEAR:
        row_copy(0, k).start()
    pair_copy(0).start()
    for j in DIRECT[:3]:
        item_copy(j).start()
    load_conf(SOON, 8)
    sums[...] = jnp.zeros_like(sums)
    add_weights(0, SOON)

    def items_of(first, last):
        return table[first:last].reshape((last - first) * 1024, K)

    def products(turn, k0, k1, first, last):
        users_here = rows[turn, k0:k1].reshape((k1 - k0) * 128, K)
        block = items_of(first, last)
        tile = conf[k0:k1, :, first * 1024:last * 1024].reshape(
            (k1 - k0) * 128, (last - first) * 1024
        ).astype(F32)
        scores = lax.dot_general(
            users_here, block, (((1,), (1,)), ((), ())), preferred_element_type=F32
        )
        residual = (tile * (scores - 1.0)).astype(BF)
        done = jnp.dot(residual, block, preferred_element_type=F32)
        return done.reshape(k1 - k0, 128, K)

    def gram_of(first, last):
        block = items_of(first, last)
        return lax.dot_general(
            block, block, (((0,), (0,)), ((), ())), preferred_element_type=F32
        )

    def rows_arrive(turn, *ks):
        for k in ks:
            if turn == 0 and k in FAR:
                row_pass(PASSED_BY[k]).wait_recv()
            else:
                row_copy(turn, OWNER_BACK[k]).wait_recv()

    rows_arrive(0, 1, 2)
    pair_copy(0).wait_recv()
    total[0:3] = products(0, 0, 3, 0, 1)
    rows_arrive(0, VIA)
    for k in PASS_ON:
        row_pass(k).start()
    for j in (2, 3, 1):
        item_copy(CHIP_BACK[j]).wait_recv()
        for n in range(4):
            if FORWARD[n][0] == j:
                on_copy(n).start()
    pair_copy(1).start()

    add_weights(SOON, 8)
    line = lax.broadcasted_iota(jnp.int32, (8, K), 0)
    own_weight = jnp.zeros((8, K), F32)
    for k in range(8):
        summed = lax.dot_general(
            jnp.ones((8, K), F32), sums[k], (((1,), (1,)), ((), ())),
            precision=HIGHEST, preferred_element_type=F32,
        )
        own_weight = jnp.where(line == owner(k), summed, own_weight)
    weight_out[...] = own_weight
    for k in NEAR:
        weight_copy(k).start()

    gram = gram_of(0, 1)
    for n in (0, 1):
        on_copy(n).wait_recv()
    on_copy(4).start()
    pair_copy(2).start()
    pair_copy(1).wait_recv()
    total[0:3] = total[0:3] + products(0, 0, 3, 1, 4)
    rows_arrive(0, *FAR)
    rows_arrive(0, 4)
    weight_copy(OWNER_BACK[VIA]).wait_recv()
    for k in PASS_ON:
        weight_pass(k).start()
    total[3:5] = products(0, 3, 5, 0, 4)
    total[5:8] = products(0, 5, 8, 0, 4)
    for n in (2, 3, 4):
        on_copy(n).wait_recv()
    pair_copy(3).start()
    pair_copy(2).wait_recv()
    total[...] = total[...] + products(0, 0, 8, 4, 5)
    gram = gram + gram_of(1, 5)

    for k in range(1, 8):
        if k in FAR:
            weight_pass(PASSED_BY[k]).wait_recv()
        elif k != VIA:
            weight_copy(OWNER_BACK[k]).wait_recv()
        own_weight = own_weight + weight_in[k]
    reciprocal = 1.0 / (own_weight + prior_weight)
    for k in range(8):
        picked = jnp.sum(jnp.where(line == owner(k), reciprocal, 0.0), axis=0, keepdims=True)
        inverse[k] = jnp.transpose(jnp.broadcast_to(picked, (128, K)))

    pair_copy(3).wait_recv()
    gram = (gram + gram_of(LATE, 8)) * (gram_coef / ITEMS)
    high = gram.astype(BF)
    low = (gram - high.astype(F32)).astype(BF)
    both = jnp.concatenate([high, low], axis=1)

    def part_of(turn, k, product):
        wide = jnp.dot(rows[turn, k], both, preferred_element_type=F32)
        return product * inverse[k] + (wide[:, :K] + wide[:, K:])

    def hand_out(turn, k, product):
        part = part_of(turn, k, product)
        parts[turn, k] = (part - SHIFT * rows[turn, k].astype(F32)).astype(BF)
        part_copy(turn, k).start()

    def step(turn, factors, gradient):
        gradient = gradient + ridge_coef * factors
        gradient = gradient + (7 * SHIFT) * rows[turn, 0].astype(F32)
        for k in FIRST_ORDER[:7]:
            part_copy(turn, OWNER_BACK[k]).wait_recv()
            gradient = gradient + shares[turn, k].astype(F32)
        return factors - jnp.dot(
            gradient, precond[...], precision=HIGHEST, preferred_element_type=F32
        )

    for k in FIRST_ORDER:
        product = total[k] + products(0, k, k + 1, LATE, 8)[0]
        if k:
            hand_out(0, k, product)
        else:
            own = part_of(0, 0, product)
    factors = step(0, users[...], own)
    rows[1, 0] = factors.astype(BF)
    for k in range(1, 8):
        row_copy(1, k).start()

    for k in SECOND_ORDER:
        if k:
            rows_arrive(1, k)
        product = products(1, k, k + 1, 0, 8)[0]
        if k:
            hand_out(1, k, product)
        else:
            own = part_of(1, 0, product)
    out[...] = step(1, factors, own)

    for g in range(len(GROUPS)):
        pair_copy(g).wait_send()
    for j in DIRECT:
        item_copy(j).wait_send()
    for n in range(len(FORWARD)):
        on_copy(n).wait_send()
    for k in PASS_ON:
        row_pass(k).wait_send()
        weight_pass(k).wait_send()
    for k in NEAR:
        weight_copy(k).wait_send()
        row_copy(0, k).wait_send()
    for k in range(1, 8):
        row_copy(1, k).wait_send()
        for turn in range(2):
            part_copy(turn, k).wait_send()


def hand_over(result, out):
    out[...] = result[...]


def shards(confidence, item_factors, user_factors, precond):
    dma = pltpu.SemaphoreType.DMA
    result = pl.pallas_call(
        kernel,
        name="user_half_step",
        out_shape=jax.ShapeDtypeStruct(user_factors.shape, F32),
        in_specs=[pl.BlockSpec(memory_space=pl.ANY)] * 4,
        out_specs=pl.BlockSpec(memory_space=pltpu.VMEM),
        scratch_shapes=[
            pltpu.VMEM((8, 128, 8192), BF),
            pltpu.VMEM((8, 1024, K), BF),
            pltpu.VMEM((128, K), F32),
            pltpu.VMEM((K, K), F32),
            pltpu.VMEM((2, 8, 128, K), BF),
            pltpu.VMEM((8, 128, K), F32),
            pltpu.VMEM((8, 128, K), F32),
            pltpu.VMEM((8, 128, K), F32),
            pltpu.VMEM((2, 8, 128, K), BF),
            pltpu.VMEM((2, 8, 128, K), BF),
            pltpu.VMEM((8, K), F32),
            pltpu.VMEM((8, 8, K), F32),
            dma((8, 8)), dma((3,)), dma((8,)), dma((8,)), dma((8,)), dma((8,)),
            dma((8,)), dma((2, 8)), dma((2, 8)), dma((2, 8)), dma((2, 8)), dma((8,)), dma((8,)),
            dma((2, 8)),
        ],
        compiler_params=pltpu.CompilerParams(
            collective_id=0, has_side_effects=True, vmem_limit_bytes=56 * 2**20
        ),
        cost_estimate=pl.CostEstimate(
            flops=4 * 2 * 1024 * 8192 * 128, bytes_accessed=17 * 2**20, transcendentals=0
        ),
    )(confidence, item_factors, user_factors, precond)
    return pl.pallas_call(
        hand_over, name="hand_over", out_shape=jax.ShapeDtypeStruct(result.shape, F32)
    )(result)


def solution(mesh):
    return jax.shard_map(
        shards,
        mesh=mesh,
        in_specs=(P("user", "item"), P(("item", "user"), None), P(("user", "item"), None), P()),
        out_specs=P(("user", "item"), None),
        check_vma=False,
    )
```
